32 devices in a mesh: group: 2 (over x), tensor: 16 (over z, y, core).
Axes of the slice: x: 2, y: 2, z: 4, core: 2. Of those that a mesh axis runs over, the one named last changes fastest.
Arguments:
- hidden: bfloat16 [8192, 1024], P('tensor', 'group'), parts along dimension 1, may hold values from -6 to 6
- input_conv_weight: bfloat16 [8192, 8192], P(None, 'tensor'), may hold values from -0.0625 to 0.0625
- input_gate_weight: bfloat16 [8192, 8192], P(None, 'tensor'), may hold values from -0.0625 to 0.0625
- convolution_taps: bfloat16 [4, 8192], P(None, 'tensor'), may hold values from -3 to 3
- convolution_bias: bfloat16 [8192], P('tensor'), may hold values from -3 to 3
- step_input_projection: bfloat16 [8192, 544], P('tensor'), may hold values from -0.0625 to 0.0625
- step_norm_gain: float32 [512], replicated, may hold values from 0.25 to 1.75
- step_size_projection: bfloat16 [512, 8192], P(None, 'tensor'), may hold values from -0.25 to 0.25
- step_size_bias: float32 [8192], P('tensor'), may hold values from -4 to -1
- decay_rates: float32 [16, 8192], P(None, 'tensor'), may hold values from 0.5 to 8
- skip: float32 [8192], P('tensor'), may hold values from 0.5 to 1.5
- output_weight: bfloat16 [8192, 8192], P('tensor'), may hold values from -0.09375 to 0.09375
- adapter_down_maps: bfloat16 [16, 8192, 64], P(None, 'tensor'), may hold values from -0.0625 to 0.0625
- adapter_up_maps: bfloat16 [16, 64, 8192], P(None, None, 'tensor'), may hold values from -0.75 to 0.75
- tenant: int32 [1024, 1], P('group'), parts along dimension 0, may hold values from 0 to 15; in each aligned block of 512 rows (0 to 511, 512 to 1023, ...) at most 128 rows name the same one
- convolution_cache: bfloat16 [3, 8192, 1024], P(None, 'tensor', 'group'), parts along dimension 2, may hold values from -6 to 6
- recurrent_cache: bfloat16 [16, 8192, 1024], P(None, 'tensor', 'group'), parts along dimension 2, may hold values from -6 to 6
- incoming_recurrent_states: bfloat16 [64, 16, 8192], P(('group', 'tensor')), parts along dimension 0, may hold values from -8 to 8
- incoming_conv_states: bfloat16 [64, 3, 8192], P(('group', 'tensor')), parts along dimension 0, may hold values from -8 to 8
- incoming_buffer_row: int32 [64], P('group'), parts along dimension 0, may hold values from 0 to 31, each once
- incoming_slot_index: int32 [64], P('group'), parts along dimension 0, may hold values from 0 to 511, as said below
Outputs:
- mixed: bfloat16 [8192, 1024], P('tensor', 'group'), parts along dimension 1
- ssm_next: bfloat16 [16, 8192, 1024], P(None, 'tensor', 'group'), parts along dimension 2
- conv_next: bfloat16 [3, 8192, 1024], P(None, 'tensor', 'group'), parts along dimension 2
The draws below stay inside these ranges and needn't reach their ends.
There are 2 independent parts, one for each index of `group`. The reference program is written for one: setup_inputs(seed, part) draws one part's arguments, and reference() takes and returns one part's arrays. A program takes and returns all parts, laid end to end along the dimension named above; an argument that names none is the same for every part. Nothing has to cross between parts.
Inputs may be any that keep to these rules, and one draw needn't show every extreme that they name: At most 128 requests have one tenant; one tenant has exactly 128. `incoming_slot_index`: distinct request slots.
All inputs are finite; a program needn't handle non-finite values.
Results may differ from the reference program's by a relative error of at most 0.008.
Values may be sent and summed in bfloat16 or wider, within the bound.
A program may use at most 192 MiB of HBM per device.

```python
import math
import jax
import jax.numpy as jnp
import numpy as np
from jax import lax

MODEL_WIDTH = 8192
INNER_HALF = 8192
N = 16
DTR = 512
KC = 4
ADAPTER_RANK = 64
TENANT_COUNT = 16
REQS = 512
MIG = 32
TENANT_ROWS = 128


def draw_incoming_slot_index(key, part):
    key = jax.random.fold_in(key, 7)
    first_key, second_key = jax.random.split(key)
    middle = jax.random.permutation(first_key, REQS - 2)[:MIG - 2] + 1
    chosen = jnp.concatenate([jnp.array([0, REQS - 1], jnp.int32), middle.astype(jnp.int32)])
    order = jax.random.permutation(second_key, MIG)
    return jnp.take(chosen, order).astype(jnp.int32)


def with_spikes(result, key, source, target, blocks, factor):
    def block_of(position):
        return (jnp.arange(result.shape[position]) // (result.shape[position] // blocks)).reshape((-1,) + (1,) * (result.ndim - 1 - position))

    first = jax.random.permutation(key, blocks)[block_of(target)]
    far = (block_of(target) + blocks // 2) % blocks
    return jnp.where((block_of(source) == first) | (block_of(source) == far), factor * result, result)


def level_of(key, dims, pieces, smallest, top_value):
    gain, own = 1.0, jax.random.fold_in(key, 6)
    for position, parts in pieces:
        steps = jnp.exp(jax.random.uniform(jax.random.fold_in(own, position), (parts,), jnp.float32, smallest / len(pieces), top_value / len(pieces)))
        gain = gain * jnp.repeat(steps, dims[position] // parts).reshape([-1 if axis == position else 1 for axis in range(len(dims))])
    return gain


def assign_block(rng, own, number, rows, amount, top, most, skew):
    ranking = jax.random.permutation(rng, amount)
    crowded, ordinary = load_shares(amount, rows * top, most, skew, True), load_shares(amount, rows * top, most, skew, False)
    places = jnp.arange(amount)

    def named(tallies, offset_by):
        used = int((tallies > 0).sum())
        fixed = max(1, used // 4)
        passed = fixed + (places - fixed + offset_by * (used - fixed)) % max(1, amount - fixed)
        return jnp.zeros((amount,), jnp.int32).at[ranking[jnp.where(places < fixed, places, passed)]].set(jnp.asarray(tallies, jnp.int32))

    tallies = jnp.where(number % 4 == 0, named(crowded, number // 4), named(ordinary, number - number // 4 - 1))
    mixed = jax.random.permutation(jax.random.fold_in(own, 3), amount)
    source_of, sink = mixed[0:amount // 2 * 2:2], mixed[1:amount // 2 * 2:2]
    room = jnp.minimum(tallies[source_of] - 1, most - tallies[sink]) // 2
    room = jnp.where((source_of == ranking[0]) | (sink == ranking[0]) | (tallies[sink] == 0), 0, jnp.maximum(room, 0))
    passed = jax.random.randint(jax.random.fold_in(own, 4), (amount // 2,), 0, 1 << 20) % (room + 1)
    tallies = tallies.at[source_of].add(-passed).at[sink].add(passed)
    members = jnp.searchsorted(jnp.cumsum(tallies), jnp.arange(rows * top), side="right").astype(jnp.int32)
    table = members.reshape(top, rows).T
    table = table[jax.random.permutation(jax.random.fold_in(own, 1), rows)]
    offset_by = jax.random.randint(jax.random.fold_in(own, 2), (rows, 1), 0, top)
    return jnp.take_along_axis(table, (jnp.arange(top)[None, :] + offset_by) % top, axis=1)


def load_shares(count, total, most, skew, full):
    portions = [(1 << 20) // math.isqrt(grade ** skew) + 1 for grade in range(1, count + 1)]
    largest = most if full else min(most, max(-(-total // count), total * portions[0] // sum(portions)))
    least = 1 if total - largest >= count - 1 else 0
    counts, surplus = [largest] + [least] * (count - 1), total - largest - least * (count - 1)
    while surplus > 0:
        movable = [i for i in range(1, count) if counts[i] < largest] or [i for i in range(1, count) if counts[i] < most]
        pool, remaining = sum([portions[i] for i in movable]), surplus
        for i in movable:
            extra = min(most - counts[i], max(1, remaining * portions[i] // pool), surplus)
            counts[i] = counts[i] + extra
            surplus = surplus - extra
    return np.array(counts)


def normal_values(rng, shape, spread, reach, cuts=(), kind=jnp.bfloat16):
    values = jax.random.normal(rng, shape, jnp.float32) * spread
    if len(cuts) > 0:
        values = level_of(rng, shape, cuts, -0.22, 0.18) * values
    return jnp.clip(values, min=-reach, max=reach).astype(kind)


def noise_with(own_key, extent, deviation, bound, pieces, heavy, held_as=jnp.bfloat16):
    values = deviation * jax.random.normal(own_key, extent, jnp.float32)
    if pieces:
        values = values * level_of(own_key, extent, pieces, -0.22, 0.18)
    return jnp.clip(with_spikes(values, jax.random.fold_in(own_key, 3), *heavy), -bound, bound).astype(held_as)


def setup_inputs(seed: int = 0, part: int = 0) -> dict:
    arg_keys = jax.random.split(jax.random.key(seed), 22)
    part_splits = jax.random.split(jax.random.fold_in(arg_keys[21], part), 22)
    hidden = normal_values(part_splits[0], (MODEL_WIDTH, REQS), 1.0, 6.0, ((0, 16),))
    input_conv_weight = normal_values(arg_keys[1], (MODEL_WIDTH, INNER_HALF), MODEL_WIDTH ** -0.5, 0.0625, ((1, 16),))
    input_gate_weight = normal_values(arg_keys[2], (MODEL_WIDTH, INNER_HALF), MODEL_WIDTH ** -0.5, 0.0625, ((1, 16),))
    convolution_taps = normal_values(arg_keys[3], (KC, INNER_HALF), 0.5, 3.0, ((1, 16),))
    convolution_bias = normal_values(arg_keys[4], (INNER_HALF,), 0.5, 3.0, ((0, 16),))
    step_input_projection = normal_values(arg_keys[5], (INNER_HALF, DTR + 2 * N), INNER_HALF ** -0.5, 0.0625, ((0, 16),))
    step_norm_gain = jnp.clip(1.0 + 0.15 * jax.random.normal(arg_keys[6], (DTR,), jnp.float32), 0.25, 1.75)
    step_size_projection = normal_values(arg_keys[7], (DTR, INNER_HALF), DTR ** -0.5, 0.25, ((1, 16),))
    step_size_bias = jnp.clip(-4.0 + 3.0 * jax.random.uniform(arg_keys[8], (INNER_HALF,), jnp.float32) ** level_of(arg_keys[8], (INNER_HALF,), ((0, 16),), -0.2, 0.2), -4.0, -1.0)
    decay_rates = jnp.clip(jnp.exp(math.log(8.0) - 2.7725887 * jax.random.uniform(arg_keys[9], (N, INNER_HALF), jnp.float32) ** level_of(arg_keys[9], (N, INNER_HALF), ((1, 16),), -0.2, 0.2)), 0.5, 8.0)
    skip = jnp.clip(0.5 + 1.0 * jax.random.uniform(arg_keys[10], (INNER_HALF,), jnp.float32) ** level_of(arg_keys[10], (INNER_HALF,), ((0, 16),), -0.2, 0.2), 0.5, 1.5)
    output_weight = noise_with(arg_keys[11], (INNER_HALF, MODEL_WIDTH), INNER_HALF ** -0.5, 0.09375, ((0, 16),), (0, 1, 16, 2.0))
    adapter_down_maps = normal_values(arg_keys[12], (TENANT_COUNT, INNER_HALF, ADAPTER_RANK), INNER_HALF ** -0.5, 0.0625, ((1, 16),))
    adapter_up_maps = normal_values(arg_keys[13], (TENANT_COUNT, ADAPTER_RANK, MODEL_WIDTH), ADAPTER_RANK ** -0.5, 0.75, ((2, 16),))
    tenant_keys = jax.random.split(jax.random.fold_in(part_splits[14], 1), REQS // REQS)
    tenant_turns = jax.random.permutation(jax.random.fold_in(part_splits[14], 3), REQS // REQS)
    tenant = jax.vmap(lambda own, number: assign_block(jax.random.fold_in(part_splits[14], 2), own, number, REQS, TENANT_COUNT, 1, TENANT_ROWS, 2))(tenant_keys, tenant_turns).reshape((REQS, 1))
    convolution_cache = normal_values(part_splits[15], (KC - 1, INNER_HALF, REQS), 1.0, 6.0, ((1, 16),))
    recurrent_cache = normal_values(part_splits[16], (N, INNER_HALF, REQS), 1.0, 6.0, ((1, 16),))
    incoming_recurrent_states = normal_values(part_splits[17], (MIG, N, INNER_HALF), 1.5, 8.0, ((0, 16),))
    incoming_conv_states = normal_values(part_splits[18], (MIG, KC - 1, INNER_HALF), 1.5, 8.0, ((0, 16),))
    incoming_buffer_row = jax.random.permutation(part_splits[19], MIG).astype(jnp.int32)
    incoming_slot_index = draw_incoming_slot_index(jax.random.fold_in(jax.random.fold_in(arg_keys[21], part), 71), part)
    return dict(hidden=hidden, input_conv_weight=input_conv_weight, input_gate_weight=input_gate_weight, convolution_taps=convolution_taps, convolution_bias=convolution_bias, step_input_projection=step_input_projection, step_norm_gain=step_norm_gain, step_size_projection=step_size_projection, step_size_bias=step_size_bias, decay_rates=decay_rates, skip=skip, output_weight=output_weight, adapter_down_maps=adapter_down_maps, adapter_up_maps=adapter_up_maps, tenant=tenant, convolution_cache=convolution_cache, recurrent_cache=recurrent_cache, incoming_recurrent_states=incoming_recurrent_states, incoming_conv_states=incoming_conv_states, incoming_buffer_row=incoming_buffer_row, incoming_slot_index=incoming_slot_index)


def slot_positions(tenant, count):
    onehot = (tenant == jnp.arange(count, dtype=jnp.int32)[None, :]).astype(jnp.int32)
    ranks = lax.optimization_barrier(jnp.sum(jnp.cumsum(onehot, axis=0) * onehot, axis=1)) - 1
    return (tenant[:, 0] * TENANT_ROWS + ranks).astype(jnp.int32)

def reference(hidden, input_conv_weight, input_gate_weight, convolution_taps, convolution_bias, step_input_projection, step_norm_gain, step_size_projection, step_size_bias, decay_rates, skip, output_weight, adapter_down_maps, adapter_up_maps, tenant, convolution_cache, recurrent_cache, incoming_recurrent_states, incoming_conv_states, incoming_buffer_row, incoming_slot_index):
    x_in = jnp.dot(input_conv_weight.T, hidden, preferred_element_type=jnp.float32)
    gate_in = jnp.dot(input_gate_weight.T, hidden, preferred_element_type=jnp.float32)
    landed_ssm = jnp.take(incoming_recurrent_states, incoming_buffer_row, axis=0)
    landed_conv = jnp.take(incoming_conv_states, incoming_buffer_row, axis=0)
    ssm_old = recurrent_cache.at[:, :, incoming_slot_index].set(jnp.transpose(landed_ssm, (1, 2, 0)))
    conv_old = convolution_cache.at[:, :, incoming_slot_index].set(jnp.transpose(landed_conv, (1, 2, 0)))
    x_low = x_in.astype(jnp.bfloat16)
    window = jnp.concatenate([conv_old, x_low[None]], axis=0)
    conv_next = window[1:]
    conv_sum = lax.optimization_barrier(jnp.sum(window.astype(jnp.float32) * convolution_taps.astype(jnp.float32)[:, :, None], axis=0))
    u_low = jax.nn.silu(conv_sum + convolution_bias.astype(jnp.float32)[:, None]).astype(jnp.bfloat16)
    mixing = jnp.dot(step_input_projection.T, u_low, preferred_element_type=jnp.float32)
    dt_low = mixing[:DTR]
    b_in = mixing[DTR:DTR + N]
    c_out = mixing[DTR + N:]
    factor = lax.rsqrt(lax.optimization_barrier(jnp.mean(dt_low * dt_low, axis=0, keepdims=True)) + 1e-06)
    dt_norm = (dt_low * factor * step_norm_gain[:, None]).astype(jnp.bfloat16)
    delta = jax.nn.softplus(jnp.dot(step_size_projection.T, dt_norm, preferred_element_type=jnp.float32) + step_size_bias[:, None])
    u_full = u_low.astype(jnp.float32)
    state = jnp.exp(-delta[None] * decay_rates[:, :, None]) * ssm_old.astype(jnp.float32) + (delta * u_full)[None] * b_in[:, None, :]
    ssm_next = state.astype(jnp.bfloat16)
    y_ssm = lax.optimization_barrier(jnp.sum(state * c_out[:, None, :], axis=0))
    y_low = ((y_ssm + skip[:, None] * u_full) * jax.nn.silu(gate_in)).astype(jnp.bfloat16)
    slot_index = slot_positions(tenant, TENANT_COUNT)
    output_padded = jnp.zeros((INNER_HALF, TENANT_COUNT * TENANT_ROWS), jnp.bfloat16).at[:, slot_index].set(y_low).reshape(INNER_HALF, TENANT_COUNT, TENANT_ROWS)
    value_lowrank = jnp.einsum('wuv,uwg->guv', output_padded.astype(jnp.float32), adapter_down_maps.astype(jnp.float32)).astype(jnp.bfloat16)
    adapter_index = jnp.einsum('ysl,sym->msl', value_lowrank.astype(jnp.float32), adapter_up_maps.astype(jnp.float32)).reshape(MODEL_WIDTH, TENANT_COUNT * TENANT_ROWS)
    adapter_index = jnp.take(adapter_index, slot_index, axis=1)
    main = jnp.dot(output_weight.T, y_low, preferred_element_type=jnp.float32)
    mixed = (main + adapter_index).astype(jnp.bfloat16)
    return (mixed, ssm_next, conv_next)
```

```python
import functools

import jax
import jax.numpy as jnp
from jax import lax
from jax.experimental import pallas as pl
from jax.experimental.pallas import tpu as pltpu
from jax.sharding import PartitionSpec as P

F32 = jnp.float32
BF16 = jnp.bfloat16
CONTRACT = (((0,), (0,)), ((), ()))
ANY = pl.BlockSpec(memory_space=pl.ANY)
VM = pl.BlockSpec(memory_space=pltpu.VMEM)
DMA = pltpu.SemaphoreType.DMA
LIMIT = 56 * 1024 * 1024


def dot0(a, b):
    return lax.dot_general(a, b, CONTRACT, preferred_element_type=F32)


def remote(src, dst, send, recv, peer):
    return pltpu.make_async_remote_copy(
        src_ref=src,
        dst_ref=dst,
        send_sem=send,
        recv_sem=recv,
        device_id={"tensor": peer},
        device_id_type=pl.DeviceIdType.MESH,
    )


def greet_all(me, n):
    barrier = pltpu.get_barrier_semaphore()

    @pl.loop(1, n)
    def _(d):
        pl.semaphore_signal(
            barrier,
            inc=1,
            device_id={"tensor": lax.rem(me + d, n)},
            device_id_type=pl.DeviceIdType.MESH,
        )

    pl.semaphore_wait(barrier, n - 1)


class Ring:
    def __init__(self, n, snake):
        self.n, self.m, self.snake = n, n // 2, snake
        self.me = lax.axis_index("tensor")
        self.core = lax.rem(self.me, 2)
        chip = self.me // 2
        if snake:
            level, side = chip // 2, lax.rem(chip, 2)
            self.pos = jnp.where(side == 0, level, self.m - 1 - level)
        else:
            self.pos = chip
        self.sibling = self.me + 1 - 2 * self.core

    def at(self, offset, core=None):
        m = self.m
        pos = lax.rem(self.pos + offset + 2 * m, m)
        if self.snake:
            chip = jnp.where(pos < m // 2, 2 * pos, 2 * (m - 1 - pos) + 1)
        else:
            chip = pos
        return chip * 2 + (self.core if core is None else core)


def gather_kernel(n, snake, h_ref, wx_hbm, wg_hbm, ssm_hbm, conv_hbm, x_ref, g_ref, ssm_out,
                  conv_out, gath, wx, wg, wsem, own_sem, rs, rr, ls, lr, ss, sr, as_, ar, cs, cr):
    ring = Ring(n, snake)
    me, m, h = ring.me, ring.m, ring.m // 2
    rows = h_ref.shape[0]
    half = rows // 2
    first, second = pl.ds(0, half), pl.ds(half, half)
    cx = pltpu.make_async_copy(wx_hbm, wx, wsem.at[0])
    cg = pltpu.make_async_copy(wg_hbm, wg, wsem.at[1])
    own = pltpu.make_async_copy(h_ref, gath.at[me], own_sem.at[0])
    own.start()
    cx.start()
    cg.start()
    width = ssm_out.shape[-1]
    keep_ssm = pltpu.make_async_copy(
        ssm_hbm.at[:, :, pl.ds(pl.multiple_of(me * width, width), width)], ssm_out.at[me],
        own_sem.at[1])
    keep_conv = pltpu.make_async_copy(conv_hbm.at[me], conv_out.at[me], own_sem.at[2])
    keep_ssm.start()
    keep_conv.start()
    x_ref[...] = jnp.zeros_like(x_ref)
    g_ref[...] = jnp.zeros_like(g_ref)
    own.wait()
    greet_all(me, n)
    right, left = ring.at(1), ring.at(-1)

    def to_right(s):
        b = gath.at[ring.at(-s)]
        return remote(b, b, rs.at[s], rr.at[s], right)

    def to_left(s):
        b = gath.at[ring.at(s)]
        return remote(b, b, ls.at[s], lr.at[s], left)

    def right_half():
        b = gath.at[ring.at(1 - h), first]
        return remote(b, b, rs.at[h - 1], rr.at[h - 1], right)

    def left_half():
        b = gath.at[ring.at(h - 1), second]
        return remote(b, b, ls.at[h - 1], lr.at[h - 1], left)

    def to_sibling(k, t):
        b = gath.at[t]
        return remote(b, b, ss.at[k], sr.at[k], ring.sibling)

    def peer_copies(d):
        t = lax.rem(me + d, n)
        return (
            remote(ssm_hbm.at[:, :, pl.ds(pl.multiple_of(t * width, width), width)],
                   ssm_out.at[me], as_.at[d], ar.at[d], t),
            remote(conv_hbm.at[t], conv_out.at[me], cs.at[d], cr.at[d], t),
        )

    def compute(t):
        block = gath[t]
        k = pl.ds(pl.multiple_of(t * rows, rows), rows)
        x_ref[...] += dot0(wx[k, :], block)
        g_ref[...] += dot0(wg[k, :], block)

    other = 1 - ring.core
    to_right(0).start()
    to_left(0).start()
    to_sibling(0, me).start()

    @pl.loop(1, n)
    def _(d):
        for c in peer_copies(d):
            c.start()

    cx.wait()
    cg.wait()
    compute(me)
    to_sibling(0, ring.sibling).wait_recv()
    compute(ring.sibling)

    def step(s, last):
        a, b = ring.at(-1 - s), ring.at(1 + s)
        remote(gath.at[a], gath.at[a], rs.at[s], rr.at[s], right).wait_recv()
        remote(gath.at[b], gath.at[b], ls.at[s], lr.at[s], left).wait_recv()
        if last:
            right_half().start()
            left_half().start()
        else:
            to_right(s + 1).start()
            to_left(s + 1).start()
        to_sibling(1 + 2 * s, a).start()
        to_sibling(2 + 2 * s, b).start()
        compute(a)
        compute(b)
        a2, b2 = ring.at(-1 - s, other), ring.at(1 + s, other)
        to_sibling(1 + 2 * s, a2).wait_recv()
        compute(a2)
        to_sibling(2 + 2 * s, b2).wait_recv()
        compute(b2)

    @pl.loop(0, h - 2)
    def _(s):
        step(s, False)

    step(h - 2, True)
    far, far2 = ring.at(h), ring.at(h, other)
    b = gath.at[far, first]
    remote(b, b, rs.at[h - 1], rr.at[h - 1], right).wait_recv()
    b = gath.at[far, second]
    remote(b, b, ls.at[h - 1], lr.at[h - 1], left).wait_recv()
    to_sibling(m - 1, far).start()
    compute(far)
    to_sibling(m - 1, far2).wait_recv()
    compute(far2)

    @pl.loop(0, h - 1)
    def _(s):
        to_right(s).wait_send()
        to_left(s).wait_send()
        to_sibling(1 + 2 * s, ring.at(-1 - s)).wait_send()
        to_sibling(2 + 2 * s, ring.at(1 + s)).wait_send()

    right_half().wait_send()
    left_half().wait_send()
    to_sibling(0, me).wait_send()
    to_sibling(m - 1, far).wait_send()
    keep_ssm.wait()
    keep_conv.wait()

    @pl.loop(1, n)
    def _(d):
        t = lax.rem(me + n - d, n)
        for c in peer_copies(d):
            c.wait_send()
        remote(ssm_out.at[t], ssm_out.at[t], as_.at[d], ar.at[d], t).wait_recv()
        remote(conv_out.at[t], conv_out.at[t], cs.at[d], cr.at[d], t).wait_recv()


def mix_kernel(n, rank, part_ref, gain_ref, dt_ref, bc_ref, recv, s1, r1, s2, r2, s3, r3):
    me = lax.axis_index("tensor")
    greet_all(me, n)

    @pl.loop(1, n)
    def _(d):
        t = lax.rem(me + d, n)
        remote(part_ref.at[t], recv.at[d], s1.at[d], r1.at[d], t).start()

    recv[0] = part_ref[me]

    @pl.loop(1, n)
    def _(d):
        remote(part_ref.at[0], recv.at[d], s1.at[d], r1.at[d], lax.rem(me + d, n)).wait()

    total = jnp.sum(recv[...].astype(F32), axis=0)
    dt = total[:, :rank]
    factor = lax.rsqrt(jnp.mean(dt * dt, axis=1, keepdims=True) + 1e-06)
    dt_ref[me] = (dt * factor * gain_ref[...]).astype(BF16)
    bc_ref[me] = total[:, rank:]

    @pl.loop(1, n)
    def _(d):
        t = lax.rem(me + d, n)
        remote(dt_ref.at[me], dt_ref.at[me], s2.at[d], r2.at[d], t).start()
        remote(bc_ref.at[me], bc_ref.at[me], s3.at[d], r3.at[d], t).start()

    @pl.loop(1, n)
    def _(d):
        t = lax.rem(me + n - d, n)
        remote(dt_ref.at[t], dt_ref.at[t], s2.at[d], r2.at[d], t).wait()
        remote(bc_ref.at[t], bc_ref.at[t], s3.at[d], r3.at[d], t).wait()


def scatter_kernel(n, snake, y_ref, w_hbm, v_ref, out_ref, v_out, w, acc, sbuf, rbuf, rsend, rrecv,
                   lsend, lrecv, vrecv, wsem, rs, rr, ls, lr, ss, sr, s1, r1, s2, r2):
    ring = Ring(n, snake)
    me, m, h = ring.me, ring.m, ring.m // 2
    rows = out_ref.shape[0]
    half = rows // 2
    first, second = pl.ds(0, half), pl.ds(half, half)
    cw = pltpu.make_async_copy(w_hbm, w, wsem.at[0])
    cw.start()
    greet_all(me, n)
    right, left = ring.at(1), ring.at(-1)
    other = 1 - ring.core

    @pl.loop(1, n)
    def _(d):
        t = lax.rem(me + d, n)
        remote(v_ref.at[t], vrecv.at[d], s1.at[d], r1.at[d], t).start()

    vrecv[0] = v_ref[me]
    cw.wait()

    def part(t):
        return dot0(w[:, pl.ds(pl.multiple_of(t * rows, rows), rows)], y_ref[...])

    def sib(k):
        return remote(sbuf.at[k], rbuf.at[k], ss.at[k], sr.at[k], ring.sibling)

    def give(k, offset):
        sbuf[k] = part(ring.at(offset, other)).astype(BF16)
        sib(k).start()

    def take(k, offset):
        acc[...] = part(ring.at(offset))
        sib(k).wait_recv()
        acc[...] += rbuf[k].astype(F32)

    def going(s, to_right):
        if to_right:
            return remote(rsend.at[s], rrecv.at[s], rs.at[s], rr.at[s], right)
        return remote(lsend.at[s], lrecv.at[s], ls.at[s], lr.at[s], left)

    def start_half(to_right):
        if to_right:
            return remote(rsend.at[0, first], rrecv.at[0, first], rs.at[0], rr.at[0], right)
        return remote(lsend.at[0, second], lrecv.at[0, second], ls.at[0], lr.at[0], left)

    give(0, h)
    take(0, h)
    rsend[0, first] = acc[first].astype(BF16)
    start_half(True).start()
    lsend[0, second] = acc[second].astype(BF16)
    start_half(False).start()

    give(1, h - 1)
    give(2, 1 - h)
    take(1, h - 1)
    start_half(True).wait_recv()
    rsend[1, first] = (acc[first] + rrecv[0, first].astype(F32)).astype(BF16)
    rsend[1, second] = acc[second].astype(BF16)
    going(1, True).start()
    take(2, 1 - h)
    start_half(False).wait_recv()
    lsend[1, second] = (acc[second] + lrecv[0, second].astype(F32)).astype(BF16)
    lsend[1, first] = acc[first].astype(BF16)
    going(1, False).start()

    @pl.loop(1, n)
    def _(d):
        remote(v_ref.at[0], vrecv.at[d], s1.at[d], r1.at[d], lax.rem(me + d, n)).wait()

    v_out[me] = jnp.sum(vrecv[...], axis=0).astype(BF16)

    @pl.loop(1, n)
    def _(d):
        remote(v_out.at[me], v_out.at[me], s2.at[d], r2.at[d], lax.rem(me + d, n)).start()

    @pl.loop(2, h)
    def _(s):
        give(2 * s - 1, h - s)
        give(2 * s, s - h)
        take(2 * s - 1, h - s)
        going(s - 1, True).wait_recv()
        rsend[s] = (acc[...] + rrecv[s - 1].astype(F32)).astype(BF16)
        going(s, True).start()
        take(2 * s, s - h)
        going(s - 1, False).wait_recv()
        lsend[s] = (acc[...] + lrecv[s - 1].astype(F32)).astype(BF16)
        going(s, False).start()

    give(m - 1, 0)
    take(m - 1, 0)
    going(h - 1, True).wait_recv()
    going(h - 1, False).wait_recv()
    out_ref[...] = acc[...] + rrecv[h - 1].astype(F32) + lrecv[h - 1].astype(F32)

    start_half(True).wait_send()
    start_half(False).wait_send()

    @pl.loop(1, h)
    def _(s):
        going(s, True).wait_send()
        going(s, False).wait_send()

    @pl.loop(0, m)
    def _(k):
        sib(k).wait_send()

    @pl.loop(1, n)
    def _(d):
        t = lax.rem(me + n - d, n)
        remote(v_out.at[t], v_out.at[t], s2.at[d], r2.at[d], t).wait()


def conv_kernel(x_ref, cache_ref, land_ref, pick_ref, hit_ref, taps_ref, bias_ref, next_ref, u_ref):
    hit = hit_ref[...] > 0
    total = bias_ref[...]
    count = cache_ref.shape[0]
    for k in range(count):
        placed = dot0(land_ref[k], pick_ref[...])
        old = jnp.where(hit, placed, cache_ref[k].astype(F32))
        total = total + old * taps_ref[:, k : k + 1]
        if k > 0:
            next_ref[k - 1] = old.astype(BF16)
    low = x_ref[...].astype(BF16)
    next_ref[count - 1] = low
    total = total + low.astype(F32) * taps_ref[:, count : count + 1]
    u_ref[...] = (total / (1.0 + jnp.exp(-total))).astype(BF16)


def state_kernel(dt_ref, proj_ref, bias_ref, decay_ref, skip_ref, u_ref, gate_ref, b_ref, c_ref,
                 cache_ref, land_ref, pick_ref, hit_ref, next_ref, y_ref):
    pre = dot0(proj_ref[...], dt_ref[...]) + bias_ref[...]
    delta = jnp.maximum(pre, 0.0) + jnp.log1p(jnp.exp(-jnp.abs(pre)))
    u = u_ref[...].astype(F32)
    du = delta * u
    hit = hit_ref[...] > 0
    total = skip_ref[...] * u
    for k in range(cache_ref.shape[0]):
        placed = dot0(land_ref[k], pick_ref[...])
        old = jnp.where(hit, placed, cache_ref[k].astype(F32))
        state = jnp.exp(-delta * decay_ref[:, k : k + 1]) * old + du * b_ref[k : k + 1, :]
        next_ref[k] = state.astype(BF16)
        total = total + state * c_ref[k : k + 1, :]
    gate = gate_ref[...]
    y_ref[...] = (total * (gate / (1.0 + jnp.exp(-gate)))).astype(BF16)


def local(n, snake, hidden, input_conv_weight, input_gate_weight, convolution_taps, convolution_bias,
          step_input_projection, step_norm_gain, step_size_projection, step_size_bias, decay_rates,
          skip, output_weight, adapter_down_maps, adapter_up_maps, tenant, convolution_cache,
          recurrent_cache, incoming_recurrent_states, incoming_conv_states, incoming_buffer_row,
          incoming_slot_index):
    rows, reqs = hidden.shape
    width, chans = input_conv_weight.shape
    rank = step_size_projection.shape[0]
    states = decay_rates.shape[0]
    taps = convolution_cache.shape[0]
    tenants, _, low_rank = adapter_down_maps.shape
    held = incoming_recurrent_states.shape[0]
    m, h = n // 2, n // 4
    share = reqs // n
    sds = jax.ShapeDtypeStruct

    def params(cid):
        return pltpu.CompilerParams(
            collective_id=cid, has_side_effects=True, vmem_limit_bytes=LIMIT)

    conv_rows = -(-held * taps // 16) * 16
    conv_in = incoming_conv_states.reshape(held * taps, n, chans).transpose(1, 0, 2)
    conv_in = jnp.pad(conv_in, ((0, 0), (0, conv_rows - held * taps), (0, 0)))

    x_in, gate_in, land_ssm, land_conv = pl.pallas_call(
        functools.partial(gather_kernel, n, snake),
        name="gather_project",
        out_shape=(sds((chans, reqs), F32), sds((chans, reqs), F32),
                   sds((n, held, states, chans), BF16), sds((n, conv_rows, chans), BF16)),
        in_specs=[VM, ANY, ANY, ANY, ANY],
        out_specs=(VM, VM, ANY, ANY),
        scratch_shapes=[
            pltpu.VMEM((n, rows, reqs), BF16), pltpu.VMEM((width, chans), BF16),
            pltpu.VMEM((width, chans), BF16), DMA((2,)), DMA((3,)),
            DMA((h,)), DMA((h,)), DMA((h,)), DMA((h,)), DMA((m,)), DMA((m,)),
            DMA((n,)), DMA((n,)), DMA((n,)), DMA((n,))],
        compiler_params=params(0),
    )(hidden, input_conv_weight, input_gate_weight, incoming_recurrent_states, conv_in)

    buffers = n * held
    land_ssm = land_ssm.reshape(buffers, states, chans).transpose(1, 0, 2)
    land_conv = land_conv[:, : held * taps].reshape(buffers, taps, chans).transpose(1, 0, 2)
    pick = ((incoming_buffer_row[:, None] == jnp.arange(buffers)[None, :]).astype(F32)).T @ (
        incoming_slot_index[:, None] == jnp.arange(reqs)[None, :]).astype(F32)
    hit = jnp.sum(pick, axis=0, keepdims=True)
    pick = pick.astype(BF16)

    eb = 128
    grid = (chans // eb,)
    whole = lambda *shape: pl.BlockSpec(shape, lambda i: (0,) * len(shape))
    rowb = lambda cols: pl.BlockSpec((eb, cols), lambda i: (i, 0))
    mid = lambda lead, cols: pl.BlockSpec((lead, eb, cols), lambda i: (0, i, 0))
    lastb = lambda lead, m_: pl.BlockSpec((lead, m_, eb), lambda i: (0, 0, i))

    conv_next, u = pl.pallas_call(
        conv_kernel,
        name="conv_step",
        grid=grid,
        out_shape=(sds((taps, chans, reqs), BF16), sds((chans, reqs), BF16)),
        in_specs=[rowb(reqs), mid(taps, reqs), lastb(taps, buffers), whole(buffers, reqs),
                  whole(1, reqs), rowb(taps + 1), rowb(1)],
        out_specs=(mid(taps, reqs), rowb(reqs)),
        compiler_params=pltpu.CompilerParams(vmem_limit_bytes=LIMIT),
    )(x_in, convolution_cache, land_conv, pick, hit, convolution_taps.astype(F32).T,
      convolution_bias.astype(F32)[:, None])

    mix_part = dot0(u, step_input_projection).astype(BF16).reshape(n, share, rank + 2 * states)
    dt_norm, bc = pl.pallas_call(
        functools.partial(mix_kernel, n, rank),
        name="mix_sum",
        out_shape=(sds((n, share, rank), BF16), sds((n, share, 2 * states), F32)),
        in_specs=[VM, VM],
        out_specs=(VM, VM),
        scratch_shapes=[pltpu.VMEM((n, share, rank + 2 * states), BF16)] + [DMA((n,))] * 6,
        compiler_params=params(1),
    )(mix_part, step_norm_gain[None, :])
    dt_norm = dt_norm.reshape(reqs, rank).T
    bc = bc.reshape(reqs, 2 * states).T

    ssm_next, y = pl.pallas_call(
        state_kernel,
        name="state_step",
        grid=grid,
        out_shape=(sds((states, chans, reqs), BF16), sds((chans, reqs), BF16)),
        in_specs=[whole(rank, reqs), pl.BlockSpec((rank, eb), lambda i: (0, i)), rowb(1),
                  rowb(states), rowb(1), rowb(reqs), rowb(reqs), whole(states, reqs),
                  whole(states, reqs), mid(states, reqs), lastb(states, buffers),
                  whole(buffers, reqs), whole(1, reqs)],
        out_specs=(mid(states, reqs), rowb(reqs)),
        compiler_params=pltpu.CompilerParams(vmem_limit_bytes=LIMIT),
    )(dt_norm, step_size_projection, step_size_bias[:, None], decay_rates.T, skip[:, None], u,
      gate_in, bc[:states], bc[states:], recurrent_cache, land_ssm, pick, hit)

    mine = tenant[:, 0][None, :] == jnp.arange(tenants, dtype=jnp.int32)[:, None]
    down = adapter_down_maps.transpose(0, 2, 1).reshape(tenants * low_rank, chans)
    v_all = jnp.dot(down, y, preferred_element_type=F32).reshape(tenants, low_rank, reqs)
    v_part = jnp.sum(jnp.where(mine[:, None, :], v_all, 0.0), axis=0)
    v_part = v_part.T.reshape(n, share, low_rank)

    block = pltpu.VMEM((h, rows, reqs), BF16)
    pairs = pltpu.VMEM((m, rows, reqs), BF16)
    main, v = pl.pallas_call(
        functools.partial(scatter_kernel, n, snake),
        name="project_scatter",
        out_shape=(sds((rows, reqs), F32), sds((n, share, low_rank), BF16)),
        in_specs=[VM, ANY, VM],
        out_specs=(VM, VM),
        scratch_shapes=[
            pltpu.VMEM((chans, width), BF16), pltpu.VMEM((rows, reqs), F32), pairs, pairs,
            block, block, block, block, pltpu.VMEM((n, share, low_rank), F32), DMA((1,)),
            DMA((h,)), DMA((h,)), DMA((h,)), DMA((h,)), DMA((m,)), DMA((m,)),
            DMA((n,)), DMA((n,)), DMA((n,)), DMA((n,))],
        compiler_params=params(2),
    )(y, output_weight, v_part)

    v = v.reshape(reqs, low_rank).T
    v_wide = jnp.where(mine[:, None, :], v[None], jnp.zeros((), BF16))
    up = adapter_up_maps.reshape(tenants * low_rank, rows)
    mixed = main + dot0(up, v_wide.reshape(tenants * low_rank, reqs))
    return mixed.astype(BF16), ssm_next, conv_next


def solution(mesh):
    placed = (
        P("tensor", "group"),
        P(None, "tensor"),
        P(None, "tensor"),
        P(None, "tensor"),
        P("tensor"),
        P("tensor", None),
        P(),
        P(None, "tensor"),
        P("tensor"),
        P(None, "tensor"),
        P("tensor"),
        P("tensor", None),
        P(None, "tensor", None),
        P(None, None, "tensor"),
        P("group", None),
        P(None, "tensor", "group"),
        P(None, "tensor", "group"),
        P(("group", "tensor"), None, None),
        P(("group", "tensor"), None, None),
        P("group"),
        P("group"),
    )
    n = mesh.shape["tensor"]
    snake = mesh.shape["group"] == 2
    return jax.shard_map(
        functools.partial(local, n, snake),
        mesh=mesh,
        in_specs=placed,
        out_specs=(P("tensor", "group"), P(None, "tensor", "group"), P(None, "tensor", "group")),
        check_vma=False,
    )
```

```python
import functools

import jax
import jax.numpy as jnp
from jax import lax
from jax.experimental import pallas as pl
from jax.experimental.pallas import tpu as pltpu
from jax.sharding import PartitionSpec as P

F32 = jnp.float32
BF16 = jnp.bfloat16
CONTRACT = (((0,), (0,)), ((), ()))
ANY = pl.BlockSpec(memory_space=pl.ANY)
VM = pl.BlockSpec(memory_space=pltpu.VMEM)
DMA = pltpu.SemaphoreType.DMA
LIMIT = 56 * 1024 * 1024


def dot0(a, b):
    return lax.dot_general(a, b, CONTRACT, preferred_element_type=F32)


def remote(src, dst, send, recv, peer):
    return pltpu.make_async_remote_copy(
        src_ref=src,
        dst_ref=dst,
        send_sem=send,
        recv_sem=recv,
        device_id={"tensor": peer},
        device_id_type=pl.DeviceIdType.MESH,
    )


def greet_all(me, n):
    barrier = pltpu.get_barrier_semaphore()

    @pl.loop(1, n)
    def _(d):
        pl.semaphore_signal(
            barrier,
            inc=1,
            device_id={"tensor": lax.rem(me + d, n)},
            device_id_type=pl.DeviceIdType.MESH,
        )

    pl.semaphore_wait(barrier, n - 1)


class Ring:
    def __init__(self, n, snake):
        self.n, self.m, self.snake = n, n // 2, snake
        self.me = lax.axis_index("tensor")
        self.core = lax.rem(self.me, 2)
        chip = self.me // 2
        if snake:
            level, side = chip // 2, lax.rem(chip, 2)
            self.pos = jnp.where(side == 0, level, self.m - 1 - level)
        else:
            self.pos = chip
        self.sibling = self.me + 1 - 2 * self.core

    def at(self, offset, core=None):
        m = self.m
        pos = lax.rem(self.pos + offset + 2 * m, m)
        if self.snake:
            chip = jnp.where(pos < m // 2, 2 * pos, 2 * (m - 1 - pos) + 1)
        else:
            chip = pos
        return chip * 2 + (self.core if core is None else core)


def gather_kernel(n, snake, h_ref, wx_hbm, wg_hbm, ssm_hbm, conv_hbm, x_ref, g_ref, ssm_out,
                  conv_out, gath, wx, wg, wsem, own_sem, rs, rr, ls, lr, ss, sr, as_, ar, cs, cr):
    ring = Ring(n, snake)
    me, m, h = ring.me, ring.m, ring.m // 2
    rows = h_ref.shape[0]
    half = rows // 2
    first, second = pl.ds(0, half), pl.ds(half, half)
    cx = pltpu.make_async_copy(wx_hbm, wx, wsem.at[0])
    cg = pltpu.make_async_copy(wg_hbm, wg, wsem.at[1])
    own = pltpu.make_async_copy(h_ref, gath.at[me], own_sem.at[0])
    own.start()
    cx.start()
    cg.start()
    width = ssm_out.shape[-1]
    keep_ssm = pltpu.make_async_copy(
        ssm_hbm.at[:, :, pl.ds(pl.multiple_of(me * width, width), width)], ssm_out.at[me],
        own_sem.at[1])
    keep_conv = pltpu.make_async_copy(conv_hbm.at[me], conv_out.at[me], own_sem.at[2])
    keep_ssm.start()
    keep_conv.start()
    x_ref[...] = jnp.zeros_like(x_ref)
    g_ref[...] = jnp.zeros_like(g_ref)
    own.wait()
    greet_all(me, n)
    right, left = ring.at(1), ring.at(-1)

    def to_right(s):
        b = gath.at[ring.at(-s)]
        return remote(b, b, rs.at[s], rr.at[s], right)

    def to_left(s):
        b = gath.at[ring.at(s)]
        return remote(b, b, ls.at[s], lr.at[s], left)

    def right_half():
        b = gath.at[ring.at(1 - h), first]
        return remote(b, b, rs.at[h - 1], rr.at[h - 1], right)

    def left_half():
        b = gath.at[ring.at(h - 1), second]
        return remote(b, b, ls.at[h - 1], lr.at[h - 1], left)

    def to_sibling(k, t):
        b = gath.at[t]
        return remote(b, b, ss.at[k], sr.at[k], ring.sibling)

    def peer_copies(d):
        t = lax.rem(me + d, n)
        return (
            remote(ssm_hbm.at[:, :, pl.ds(pl.multiple_of(t * width, width), width)],
                   ssm_out.at[me], as_.at[d], ar.at[d], t),
            remote(conv_hbm.at[t], conv_out.at[me], cs.at[d], cr.at[d], t),
        )

    def compute(t):
        block = gath[t]
        k = pl.ds(pl.multiple_of(t * rows, rows), rows)
        x_ref[...] += dot0(wx[k, :], block)
        g_ref[...] += dot0(wg[k, :], block)

    other = 1 - ring.core
    to_right(0).start()
    to_left(0).start()
    to_sibling(0, me).start()

    @pl.loop(1, n)
    def _(d):
        for c in peer_copies(d):
            c.start()

    cx.wait()
    cg.wait()
    compute(me)
    to_sibling(0, ring.sibling).wait_recv()
    compute(ring.sibling)

    def step(s, last):
        a, b = ring.at(-1 - s), ring.at(1 + s)
        remote(gath.at[a], gath.at[a], rs.at[s], rr.at[s], right).wait_recv()
        remote(gath.at[b], gath.at[b], ls.at[s], lr.at[s], left).wait_recv()
        if last:
            right_half().start()
            left_half().start()
        else:
            to_right(s + 1).start()
            to_left(s + 1).start()
        to_sibling(1 + 2 * s, a).start()
        to_sibling(2 + 2 * s, b).start()
        compute(a)
        compute(b)
        a2, b2 = ring.at(-1 - s, other), ring.at(1 + s, other)
        to_sibling(1 + 2 * s, a2).wait_recv()
        compute(a2)
        to_sibling(2 + 2 * s, b2).wait_recv()
        compute(b2)

    @pl.loop(0, h - 2)
    def _(s):
        step(s, False)

    step(h - 2, True)
    far, far2 = ring.at(h), ring.at(h, other)
    b = gath.at[far, first]
    remote(b, b, rs.at[h - 1], rr.at[h - 1], right).wait_recv()
    b = gath.at[far, second]
    remote(b, b, ls.at[h - 1], lr.at[h - 1], left).wait_recv()
    to_sibling(m - 1, far).start()
    compute(far)
    to_sibling(m - 1, far2).wait_recv()
    compute(far2)

    @pl.loop(0, h - 1)
    def _(s):
        to_right(s).wait_send()
        to_left(s).wait_send()
        to_sibling(1 + 2 * s, ring.at(-1 - s)).wait_send()
        to_sibling(2 + 2 * s, ring.at(1 + s)).wait_send()

    right_half().wait_send()
    left_half().wait_send()
    to_sibling(0, me).wait_send()
    to_sibling(m - 1, far).wait_send()
    keep_ssm.wait()
    keep_conv.wait()

    @pl.loop(1, n)
    def _(d):
        t = lax.rem(me + n - d, n)
        for c in peer_copies(d):
            c.wait_send()
        remote(ssm_out.at[t], ssm_out.at[t], as_.at[d], ar.at[d], t).wait_recv()
        remote(conv_out.at[t], conv_out.at[t], cs.at[d], cr.at[d], t).wait_recv()


def mix_kernel(n, rank, part_ref, gain_ref, out_ref, pair, recv, s0, r0, s1, r1, s2, r2, s3, r3):
    me = lax.axis_index("tensor")
    m = n // 2
    core = lax.rem(me, 2)
    chip = me // 2
    sibling = me + 1 - 2 * core

    def peer(d):
        return lax.rem(chip + d, m) * 2 + core

    barrier = pltpu.get_barrier_semaphore()
    pl.semaphore_signal(barrier, inc=1, device_id={"tensor": sibling},
                        device_id_type=pl.DeviceIdType.MESH)

    @pl.loop(1, m)
    def _(d):
        pl.semaphore_signal(barrier, inc=1, device_id={"tensor": peer(d)},
                            device_id_type=pl.DeviceIdType.MESH)

    pl.semaphore_wait(barrier, m)

    swap = remote(part_ref.at[:, 1 - core], pair, s0.at[0], r0.at[0], sibling)
    swap.start()
    swap.wait()

    @pl.loop(0, m)
    def _(d):
        q = lax.rem(chip + d, m)
        recv[d] = (part_ref[q, core].astype(F32) + pair[q].astype(F32)).astype(BF16)

    @pl.loop(1, m)
    def _(d):
        remote(recv.at[d], recv.at[m + d], s1.at[d], r1.at[d], peer(d)).start()

    @pl.loop(1, m)
    def _(d):
        remote(recv.at[d], recv.at[m + d], s1.at[d], r1.at[d], peer(d)).wait()

    total = recv[0].astype(F32) + jnp.sum(recv[pl.ds(m + 1, m - 1)].astype(F32), axis=0)
    dt = total[:, :rank]
    factor = lax.rsqrt(jnp.mean(dt * dt, axis=1, keepdims=True) + 1e-06)
    out_ref[me, :, pl.ds(0, rank)] = (dt * factor * gain_ref[...]).astype(BF16)
    out_ref[me, :, pl.ds(rank, total.shape[1] - rank)] = total[:, rank:].astype(BF16)

    def forward(d, t):
        return remote(out_ref.at[t], out_ref.at[t], s3.at[d], r3.at[d], sibling)

    @pl.loop(1, m)
    def _(d):
        remote(out_ref.at[me], out_ref.at[me], s2.at[d], r2.at[d], peer(d)).start()

    forward(0, me).start()

    @pl.loop(1, m)
    def _(d):
        t = peer(m - d)
        remote(out_ref.at[t], out_ref.at[t], s2.at[d], r2.at[d], t).wait_recv()
        forward(d, t).start()

    @pl.loop(0, m)
    def _(d):
        t = peer(m - d)
        forward(d, t).wait_send()
        forward(d, t + 1 - 2 * core).wait_recv()

    @pl.loop(1, m)
    def _(d):
        remote(out_ref.at[me], out_ref.at[me], s2.at[d], r2.at[d], peer(d)).wait_send()


def scatter_kernel(n, snake, y_ref, w_hbm, down_ref, up_ref, tenant_ref, out_ref, w, acc, more, v_ref,
                   v_out, sbuf, rbuf, rsend, rrecv,
                   lsend, lrecv, vrecv, wsem, rs, rr, ls, lr, ss, sr, s1, r1, s2, r2):
    ring = Ring(n, snake)
    me, m, h = ring.me, ring.m, ring.m // 2
    rows = out_ref.shape[0]
    half = rows // 2
    first, second = pl.ds(0, half), pl.ds(half, half)
    cw = pltpu.make_async_copy(w_hbm, w, wsem.at[0])
    cw.start()
    greet_all(me, n)
    right, left = ring.at(1), ring.at(-1)
    other = 1 - ring.core

    cw.wait()

    def part(t):
        return dot0(w[:, pl.ds(pl.multiple_of(t * rows, rows), rows)], y_ref[...])

    def sib(k):
        return remote(sbuf.at[k], rbuf.at[k], ss.at[k], sr.at[k], ring.sibling)

    def give(k, offset):
        sbuf[k] = part(ring.at(offset, other)).astype(BF16)
        sib(k).start()

    def take(k, offset):
        acc[...] = part(ring.at(offset))
        sib(k).wait_recv()
        acc[...] += rbuf[k].astype(F32)

    def going(s, to_right):
        if to_right:
            return remote(rsend.at[s], rrecv.at[s], rs.at[s], rr.at[s], right)
        return remote(lsend.at[s], lrecv.at[s], ls.at[s], lr.at[s], left)

    def start_half(to_right):
        if to_right:
            return remote(rsend.at[0, first], rrecv.at[0, first], rs.at[0], rr.at[0], right)
        return remote(lsend.at[0, second], lrecv.at[0, second], ls.at[0], lr.at[0], left)

    give(0, h)
    take(0, h)
    rsend[0, first] = acc[first].astype(BF16)
    start_half(True).start()
    lsend[0, second] = acc[second].astype(BF16)
    start_half(False).start()

    _, share, low = v_ref.shape
    batch = 4 * low
    count = down_ref.shape[0] // batch

    def down(i, total):
        every = jnp.dot(down_ref[pl.ds(pl.multiple_of(i * batch, batch), batch), :], y_ref[...],
                        preferred_element_type=F32)
        for j in range(4):
            total = total + jnp.where(tenant_ref[...] == 4 * i + j, every[j * low : (j + 1) * low], 0.0)
        return total

    v_mine = lax.fori_loop(0, count, down, jnp.zeros((low, y_ref.shape[1]), F32))
    v_ref[...] = v_mine.T.reshape(n, share, low)
    vrecv[0] = v_ref[me]

    @pl.loop(1, n)
    def _(d):
        t = lax.rem(me + d, n)
        remote(v_ref.at[t], vrecv.at[d], s1.at[d], r1.at[d], t).start()

    give(1, h - 1)
    give(2, 1 - h)
    take(1, h - 1)
    start_half(True).wait_recv()
    rsend[1, first] = (acc[first] + rrecv[0, first].astype(F32)).astype(BF16)
    rsend[1, second] = acc[second].astype(BF16)
    going(1, True).start()
    take(2, 1 - h)
    start_half(False).wait_recv()
    lsend[1, second] = (acc[second] + lrecv[0, second].astype(F32)).astype(BF16)
    lsend[1, first] = acc[first].astype(BF16)
    going(1, False).start()

    @pl.loop(1, n)
    def _(d):
        remote(v_ref.at[0], vrecv.at[d], s1.at[d], r1.at[d], lax.rem(me + d, n)).wait()

    v_out[me] = jnp.sum(vrecv[...], axis=0).astype(BF16)

    @pl.loop(1, n)
    def _(d):
        remote(v_out.at[me], v_out.at[me], s2.at[d], r2.at[d], lax.rem(me + d, n)).start()

    @pl.loop(2, h)
    def _(s):
        give(2 * s - 1, h - s)
        give(2 * s, s - h)
        take(2 * s - 1, h - s)
        going(s - 1, True).wait_recv()
        rsend[s] = (acc[...] + rrecv[s - 1].astype(F32)).astype(BF16)
        going(s, True).start()
        take(2 * s, s - h)
        going(s - 1, False).wait_recv()
        lsend[s] = (acc[...] + lrecv[s - 1].astype(F32)).astype(BF16)
        going(s, False).start()

    give(m - 1, 0)

    @pl.loop(1, n)
    def _(d):
        t = lax.rem(me + n - d, n)
        remote(v_out.at[t], v_out.at[t], s2.at[d], r2.at[d], t).wait()

    v_all = v_out[...].astype(F32).reshape(n * share, low).T
    more[...] = jnp.zeros_like(more)

    @pl.loop(0, count)
    def _(i):
        wide = jnp.concatenate(
            [jnp.where(tenant_ref[...] == 4 * i + j, v_all, 0.0) for j in range(4)], axis=0)
        more[...] += dot0(up_ref[pl.ds(pl.multiple_of(i * batch, batch), batch), :], wide.astype(BF16))

    take(m - 1, 0)
    more[...] += acc[...]
    going(h - 1, True).wait_recv()
    going(h - 1, False).wait_recv()
    out_ref[...] = (more[...] + rrecv[h - 1].astype(F32) + lrecv[h - 1].astype(F32)).astype(BF16)

    start_half(True).wait_send()
    start_half(False).wait_send()

    @pl.loop(1, h)
    def _(s):
        going(s, True).wait_send()
        going(s, False).wait_send()

    @pl.loop(0, m)
    def _(k):
        sib(k).wait_send()


def conv_kernel(x_ref, cache_ref, land_ref, pick_ref, hit_ref, taps_ref, bias_ref, next_ref, u_ref):
    hit = hit_ref[...] > 0
    total = bias_ref[...]
    count = cache_ref.shape[0]
    for k in range(count):
        placed = dot0(land_ref[k], pick_ref[...])
        old = jnp.where(hit, placed, cache_ref[k].astype(F32))
        total = total + old * taps_ref[:, k : k + 1]
        if k > 0:
            next_ref[k - 1] = old.astype(BF16)
    low = x_ref[...].astype(BF16)
    next_ref[count - 1] = low
    total = total + low.astype(F32) * taps_ref[:, count : count + 1]
    u_ref[...] = (total / (1.0 + jnp.exp(-total))).astype(BF16)


def state_kernel(dt_ref, proj_ref, bias_ref, decay_ref, skip_ref, u_ref, gate_ref,
                 cache_ref, land_ref, pick_ref, hit_ref, next_ref, y_ref):
    rank, states = proj_ref.shape[0], cache_ref.shape[0]
    pre = dot0(proj_ref[...], dt_ref[pl.ds(0, rank), :]) + bias_ref[...]
    b_in = dt_ref[pl.ds(rank, states), :].astype(F32)
    c_out = dt_ref[pl.ds(rank + states, states), :].astype(F32)
    delta = jnp.maximum(pre, 0.0) + jnp.log1p(jnp.exp(-jnp.abs(pre)))
    u = u_ref[...].astype(F32)
    du = delta * u
    hit = hit_ref[...] > 0
    total = skip_ref[...] * u
    for k in range(cache_ref.shape[0]):
        placed = dot0(land_ref[k], pick_ref[...])
        old = jnp.where(hit, placed, cache_ref[k].astype(F32))
        state = jnp.exp(-delta * decay_ref[:, k : k + 1]) * old + du * b_in[k : k + 1, :]
        next_ref[k] = state.astype(BF16)
        total = total + state * c_out[k : k + 1, :]
    gate = gate_ref[...]
    y_ref[...] = (total * (gate / (1.0 + jnp.exp(-gate)))).astype(BF16)


def local(n, snake, hidden, input_conv_weight, input_gate_weight, convolution_taps, convolution_bias,
          step_input_projection, step_norm_gain, step_size_projection, step_size_bias, decay_rates,
          skip, output_weight, adapter_down_maps, adapter_up_maps, tenant, convolution_cache,
          recurrent_cache, incoming_recurrent_states, incoming_conv_states, incoming_buffer_row,
          incoming_slot_index):
    rows, reqs = hidden.shape
    width, chans = input_conv_weight.shape
    rank = step_size_projection.shape[0]
    states = decay_rates.shape[0]
    taps = convolution_cache.shape[0]
    tenants, _, low_rank = adapter_down_maps.shape
    held = incoming_recurrent_states.shape[0]
    m, h = n // 2, n // 4
    share = reqs // n
    sds = jax.ShapeDtypeStruct

    def params(cid):
        return pltpu.CompilerParams(
            collective_id=cid, has_side_effects=True, vmem_limit_bytes=LIMIT)

    conv_rows = -(-held * taps // 16) * 16
    conv_in = incoming_conv_states.reshape(held * taps, n, chans).transpose(1, 0, 2)
    conv_in = jnp.pad(conv_in, ((0, 0), (0, conv_rows - held * taps), (0, 0)))

    x_in, gate_in, land_ssm, land_conv = pl.pallas_call(
        functools.partial(gather_kernel, n, snake),
        name="gather_project",
        out_shape=(sds((chans, reqs), F32), sds((chans, reqs), F32),
                   sds((n, held, states, chans), BF16), sds((n, conv_rows, chans), BF16)),
        in_specs=[VM, ANY, ANY, ANY, ANY],
        out_specs=(VM, VM, ANY, ANY),
        scratch_shapes=[
            pltpu.VMEM((n, rows, reqs), BF16), pltpu.VMEM((width, chans), BF16),
            pltpu.VMEM((width, chans), BF16), DMA((2,)), DMA((3,)),
            DMA((h,)), DMA((h,)), DMA((h,)), DMA((h,)), DMA((m,)), DMA((m,)),
            DMA((n,)), DMA((n,)), DMA((n,)), DMA((n,))],
        compiler_params=params(0),
    )(hidden, input_conv_weight, input_gate_weight, incoming_recurrent_states, conv_in)

    buffers = n * held
    land_ssm = land_ssm.reshape(buffers, states, chans).transpose(1, 0, 2)
    land_conv = land_conv[:, : held * taps].reshape(buffers, taps, chans).transpose(1, 0, 2)
    pick = ((incoming_buffer_row[:, None] == jnp.arange(buffers)[None, :]).astype(F32)).T @ (
        incoming_slot_index[:, None] == jnp.arange(reqs)[None, :]).astype(F32)
    hit = jnp.sum(pick, axis=0, keepdims=True)
    pick = pick.astype(BF16)

    eb = 128
    grid = (chans // eb,)
    whole = lambda *shape: pl.BlockSpec(shape, lambda i: (0,) * len(shape))
    rowb = lambda cols: pl.BlockSpec((eb, cols), lambda i: (i, 0))
    mid = lambda lead, cols: pl.BlockSpec((lead, eb, cols), lambda i: (0, i, 0))
    lastb = lambda lead, m_: pl.BlockSpec((lead, m_, eb), lambda i: (0, 0, i))

    conv_next, u = pl.pallas_call(
        conv_kernel,
        name="conv_step",
        grid=grid,
        out_shape=(sds((taps, chans, reqs), BF16), sds((chans, reqs), BF16)),
        in_specs=[rowb(reqs), mid(taps, reqs), lastb(taps, buffers), whole(buffers, reqs),
                  whole(1, reqs), rowb(taps + 1), rowb(1)],
        out_specs=(mid(taps, reqs), rowb(reqs)),
        compiler_params=pltpu.CompilerParams(vmem_limit_bytes=LIMIT),
    )(x_in, convolution_cache, land_conv, pick, hit, convolution_taps.astype(F32).T,
      convolution_bias.astype(F32)[:, None])

    outs = rank + 2 * states
    mix_part = dot0(u, step_input_projection).astype(BF16).reshape(m, 2, share, outs)
    mixed_in = pl.pallas_call(
        functools.partial(mix_kernel, n, rank),
        name="mix_sum",
        out_shape=sds((n, share, outs), BF16),
        in_specs=[VM, VM],
        out_specs=VM,
        scratch_shapes=[pltpu.VMEM((m, share, outs), BF16), pltpu.VMEM((n, share, outs), BF16),
                        DMA((1,)), DMA((1,))] + [DMA((m,))] * 6,
        compiler_params=params(1),
    )(mix_part, step_norm_gain[None, :])
    mixed_in = mixed_in.reshape(reqs, outs).T

    ssm_next, y = pl.pallas_call(
        state_kernel,
        name="state_step",
        grid=grid,
        out_shape=(sds((states, chans, reqs), BF16), sds((chans, reqs), BF16)),
        in_specs=[whole(outs, reqs), pl.BlockSpec((rank, eb), lambda i: (0, i)), rowb(1),
                  rowb(states), rowb(1), rowb(reqs), rowb(reqs), mid(states, reqs), lastb(states, buffers),
                  whole(buffers, reqs), whole(1, reqs)],
        out_specs=(mid(states, reqs), rowb(reqs)),
        compiler_params=pltpu.CompilerParams(vmem_limit_bytes=LIMIT),
    )(mixed_in, step_size_projection, step_size_bias[:, None], decay_rates.T, skip[:, None], u,
      gate_in, recurrent_cache, land_ssm, pick, hit)

    down = adapter_down_maps.transpose(0, 2, 1).reshape(tenants * low_rank, chans)
    up = adapter_up_maps.reshape(tenants * low_rank, rows)
    block = pltpu.VMEM((h, rows, reqs), BF16)
    pairs = pltpu.VMEM((m, rows, reqs), BF16)
    mixed = pl.pallas_call(
        functools.partial(scatter_kernel, n, snake),
        name="project_scatter",
        out_shape=sds((rows, reqs), BF16),
        in_specs=[VM, ANY, VM, VM, VM],
        out_specs=VM,
        scratch_shapes=[
            pltpu.VMEM((chans, width), BF16), pltpu.VMEM((rows, reqs), F32),
            pltpu.VMEM((rows, reqs), F32), pltpu.VMEM((n, share, low_rank), F32),
            pltpu.VMEM((n, share, low_rank), BF16), pairs, pairs,
            block, block, block, block, pltpu.VMEM((n, share, low_rank), F32), DMA((1,)),
            DMA((h,)), DMA((h,)), DMA((h,)), DMA((h,)), DMA((m,)), DMA((m,)),
            DMA((n,)), DMA((n,)), DMA((n,)), DMA((n,))],
        compiler_params=params(2),
    )(y, output_weight, down, up, tenant.reshape(1, reqs))
    return mixed, ssm_next, conv_next


def solution(mesh):
    placed = (
        P("tensor", "group"),
        P(None, "tensor"),
        P(None, "tensor"),
        P(None, "tensor"),
        P("tensor"),
        P("tensor", None),
        P(),
        P(None, "tensor"),
        P("tensor"),
        P(None, "tensor"),
        P("tensor"),
        P("tensor", None),
        P(None, "tensor", None),
        P(None, None, "tensor"),
        P("group", None),
        P(None, "tensor", "group"),
        P(None, "tensor", "group"),
        P(("group", "tensor"), None, None),
        P(("group", "tensor"), None, None),
        P("group"),
        P("group"),
    )
    n = mesh.shape["tensor"]
    snake = mesh.shape["group"] == 2
    return jax.shard_map(
        functools.partial(local, n, snake),
        mesh=mesh,
        in_specs=placed,
        out_specs=(P("tensor", "group"), P(None, "tensor", "group"), P(None, "tensor", "group")),
        check_vma=False,
    )
```

```python
import functools

import jax
import jax.numpy as jnp
from jax import lax
from jax.experimental import pallas as pl
from jax.experimental.pallas import tpu as pltpu
from jax.sharding import PartitionSpec as P

F32 = jnp.float32
BF16 = jnp.bfloat16
CONTRACT = (((0,), (0,)), ((), ()))
ANY = pl.BlockSpec(memory_space=pl.ANY)
VM = pl.BlockSpec(memory_space=pltpu.VMEM)
DMA = pltpu.SemaphoreType.DMA
LIMIT = 56 * 1024 * 1024


def dot0(a, b):
    return lax.dot_general(a, b, CONTRACT, preferred_element_type=F32)


def remote(src, dst, send, recv, peer):
    return pltpu.make_async_remote_copy(
        src_ref=src,
        dst_ref=dst,
        send_sem=send,
        recv_sem=recv,
        device_id={"tensor": peer},
        device_id_type=pl.DeviceIdType.MESH,
    )


def greet_all(me, n):
    barrier = pltpu.get_barrier_semaphore()

    @pl.loop(1, n)
    def _(d):
        pl.semaphore_signal(
            barrier,
            inc=1,
            device_id={"tensor": lax.rem(me + d, n)},
            device_id_type=pl.DeviceIdType.MESH,
        )

    pl.semaphore_wait(barrier, n - 1)


class Ring:
    def __init__(self, n, snake):
        self.n, self.m, self.snake = n, n // 2, snake
        self.me = lax.axis_index("tensor")
        self.core = lax.rem(self.me, 2)
        chip = self.me // 2
        if snake:
            level, side = chip // 2, lax.rem(chip, 2)
            self.pos = jnp.where(side == 0, level, self.m - 1 - level)
        else:
            self.pos = chip
        self.sibling = self.me + 1 - 2 * self.core

    def at(self, offset, core=None):
        m = self.m
        pos = lax.rem(self.pos + offset + 2 * m, m)
        if self.snake:
            chip = jnp.where(pos < m // 2, 2 * pos, 2 * (m - 1 - pos) + 1)
        else:
            chip = pos
        return chip * 2 + (self.core if core is None else core)


def gather_kernel(n, snake, h_ref, wx_hbm, wg_hbm, ssm_hbm, conv_hbm, x_ref, g_ref, ssm_out,
                  conv_out, gath, wx, wg, wsem, own_sem, rs, rr, ls, lr, ss, sr, as_, ar, cs, cr):
    ring = Ring(n, snake)
    me, m, h = ring.me, ring.m, ring.m // 2
    rows = h_ref.shape[0]
    half = rows // 2
    first, second = pl.ds(0, half), pl.ds(half, half)
    cx = pltpu.make_async_copy(wx_hbm, wx, wsem.at[0])
    cg = pltpu.make_async_copy(wg_hbm, wg, wsem.at[1])
    own = pltpu.make_async_copy(h_ref, gath.at[me], own_sem.at[0])
    own.start()
    cx.start()
    cg.start()
    width = ssm_out.shape[-1]
    keep_ssm = pltpu.make_async_copy(
        ssm_hbm.at[:, :, pl.ds(pl.multiple_of(me * width, width), width)], ssm_out.at[me],
        own_sem.at[1])
    keep_conv = pltpu.make_async_copy(conv_hbm.at[me], conv_out.at[me], own_sem.at[2])
    keep_ssm.start()
    keep_conv.start()
    x_ref[...] = jnp.zeros_like(x_ref)
    g_ref[...] = jnp.zeros_like(g_ref)
    own.wait()
    greet_all(me, n)
    right, left = ring.at(1), ring.at(-1)

    def to_right(s):
        b = gath.at[ring.at(-s)]
        return remote(b, b, rs.at[s], rr.at[s], right)

    def to_left(s):
        b = gath.at[ring.at(s)]
        return remote(b, b, ls.at[s], lr.at[s], left)

    def right_half():
        b = gath.at[ring.at(1 - h), first]
        return remote(b, b, rs.at[h - 1], rr.at[h - 1], right)

    def left_half():
        b = gath.at[ring.at(h - 1), second]
        return remote(b, b, ls.at[h - 1], lr.at[h - 1], left)

    def to_sibling(k, t):
        b = gath.at[t]
        return remote(b, b, ss.at[k], sr.at[k], ring.sibling)

    def peer_copies(d):
        t = lax.rem(me + d, n)
        return (
            remote(ssm_hbm.at[:, :, pl.ds(pl.multiple_of(t * width, width), width)],
                   ssm_out.at[me], as_.at[d], ar.at[d], t),
            remote(conv_hbm.at[t], conv_out.at[me], cs.at[d], cr.at[d], t),
        )

    def compute(t):
        block = gath[t]
        k = pl.ds(pl.multiple_of(t * rows, rows), rows)
        x_ref[...] += dot0(wx[k, :], block)
        g_ref[...] += dot0(wg[k, :], block)

    other = 1 - ring.core
    to_right(0).start()
    to_left(0).start()
    to_sibling(0, me).start()

    @pl.loop(1, n)
    def _(d):
        for c in peer_copies(d):
            c.start()

    cx.wait()
    cg.wait()
    compute(me)
    to_sibling(0, ring.sibling).wait_recv()
    compute(ring.sibling)

    def step(s, last):
        a, b = ring.at(-1 - s), ring.at(1 + s)
        remote(gath.at[a], gath.at[a], rs.at[s], rr.at[s], right).wait_recv()
        (right_half() if last else to_right(s + 1)).start()
        to_sibling(1 + 2 * s, a).start()
        remote(gath.at[b], gath.at[b], ls.at[s], lr.at[s], left).wait_recv()
        (left_half() if last else to_left(s + 1)).start()
        to_sibling(2 + 2 * s, b).start()
        compute(a)
        compute(b)
        a2, b2 = ring.at(-1 - s, other), ring.at(1 + s, other)
        to_sibling(1 + 2 * s, a2).wait_recv()
        compute(a2)
        to_sibling(2 + 2 * s, b2).wait_recv()
        compute(b2)

    @pl.loop(0, h - 2)
    def _(s):
        step(s, False)

    step(h - 2, True)
    far, far2 = ring.at(h), ring.at(h, other)
    b = gath.at[far, first]
    remote(b, b, rs.at[h - 1], rr.at[h - 1], right).wait_recv()
    b = gath.at[far, second]
    remote(b, b, ls.at[h - 1], lr.at[h - 1], left).wait_recv()
    to_sibling(m - 1, far).start()
    compute(far)
    to_sibling(m - 1, far2).wait_recv()
    compute(far2)

    @pl.loop(0, h - 1)
    def _(s):
        to_right(s).wait_send()
        to_left(s).wait_send()
        to_sibling(1 + 2 * s, ring.at(-1 - s)).wait_send()
        to_sibling(2 + 2 * s, ring.at(1 + s)).wait_send()

    right_half().wait_send()
    left_half().wait_send()
    to_sibling(0, me).wait_send()
    to_sibling(m - 1, far).wait_send()
    keep_ssm.wait()
    keep_conv.wait()

    @pl.loop(1, n)
    def _(d):
        t = lax.rem(me + n - d, n)
        for c in peer_copies(d):
            c.wait_send()
        remote(ssm_out.at[t], ssm_out.at[t], as_.at[d], ar.at[d], t).wait_recv()
        remote(conv_out.at[t], conv_out.at[t], cs.at[d], cr.at[d], t).wait_recv()


def mix_kernel(n, rank, part_ref, gain_ref, out_ref, pair, recv, s0, r0, s1, r1, s2, r2, s3, r3):
    me = lax.axis_index("tensor")
    m = n // 2
    core = lax.rem(me, 2)
    chip = me // 2
    sibling = me + 1 - 2 * core

    def peer(d):
        return lax.rem(chip + d, m) * 2 + core

    barrier = pltpu.get_barrier_semaphore()
    pl.semaphore_signal(barrier, inc=1, device_id={"tensor": sibling},
                        device_id_type=pl.DeviceIdType.MESH)

    @pl.loop(1, m)
    def _(d):
        pl.semaphore_signal(barrier, inc=1, device_id={"tensor": peer(d)},
                            device_id_type=pl.DeviceIdType.MESH)

    pl.semaphore_wait(barrier, m)

    swap = remote(part_ref.at[:, 1 - core], pair, s0.at[0], r0.at[0], sibling)
    swap.start()
    swap.wait()

    @pl.loop(0, m)
    def _(d):
        q = lax.rem(chip + d, m)
        recv[d] = (part_ref[q, core].astype(F32) + pair[q].astype(F32)).astype(BF16)

    @pl.loop(1, m)
    def _(d):
        remote(recv.at[d], recv.at[m + d], s1.at[d], r1.at[d], peer(d)).start()

    @pl.loop(1, m)
    def _(d):
        remote(recv.at[d], recv.at[m + d], s1.at[d], r1.at[d], peer(d)).wait()

    total = recv[0].astype(F32) + jnp.sum(recv[pl.ds(m + 1, m - 1)].astype(F32), axis=0)
    dt = total[:, :rank]
    factor = lax.rsqrt(jnp.mean(dt * dt, axis=1, keepdims=True) + 1e-06)
    out_ref[me, :, pl.ds(0, rank)] = (dt * factor * gain_ref[...]).astype(BF16)
    out_ref[me, :, pl.ds(rank, total.shape[1] - rank)] = total[:, rank:].astype(BF16)

    def forward(d, t):
        return remote(out_ref.at[t], out_ref.at[t], s3.at[d], r3.at[d], sibling)

    @pl.loop(1, m)
    def _(d):
        remote(out_ref.at[me], out_ref.at[me], s2.at[d], r2.at[d], peer(d)).start()

    forward(0, me).start()

    @pl.loop(1, m)
    def _(d):
        t = peer(m - d)
        remote(out_ref.at[t], out_ref.at[t], s2.at[d], r2.at[d], t).wait_recv()
        forward(d, t).start()

    @pl.loop(0, m)
    def _(d):
        t = peer(m - d)
        forward(d, t).wait_send()
        forward(d, t + 1 - 2 * core).wait_recv()

    @pl.loop(1, m)
    def _(d):
        remote(out_ref.at[me], out_ref.at[me], s2.at[d], r2.at[d], peer(d)).wait_send()


def scatter_kernel(n, snake, y_ref, w_hbm, down_ref, up_ref, tenant_ref, out_ref, w, acc, more, v_ref,
                   v_out, sbuf, rbuf, rsend, rrecv,
                   lsend, lrecv, vrecv, wsem, rs, rr, ls, lr, ss, sr, s1, r1, s2, r2):
    ring = Ring(n, snake)
    me, m, h = ring.me, ring.m, ring.m // 2
    rows = out_ref.shape[0]
    half = rows // 2
    first, second = pl.ds(0, half), pl.ds(half, half)
    cw = pltpu.make_async_copy(w_hbm, w, wsem.at[0])
    cw.start()
    greet_all(me, n)
    right, left = ring.at(1), ring.at(-1)
    other = 1 - ring.core

    cw.wait()

    def part(t):
        return dot0(w[:, pl.ds(pl.multiple_of(t * rows, rows), rows)], y_ref[...])

    def sib(k):
        return remote(sbuf.at[k], rbuf.at[k], ss.at[k], sr.at[k], ring.sibling)

    def give(k, offset):
        sbuf[k] = part(ring.at(offset, other)).astype(BF16)
        sib(k).start()

    def take(k, offset):
        acc[...] = part(ring.at(offset))
        sib(k).wait_recv()
        acc[...] += rbuf[k].astype(F32)

    def going(s, to_right):
        if to_right:
            return remote(rsend.at[s], rrecv.at[s], rs.at[s], rr.at[s], right)
        return remote(lsend.at[s], lrecv.at[s], ls.at[s], lr.at[s], left)

    def start_half(to_right):
        if to_right:
            return remote(rsend.at[0, first], rrecv.at[0, first], rs.at[0], rr.at[0], right)
        return remote(lsend.at[0, second], lrecv.at[0, second], ls.at[0], lr.at[0], left)

    give(0, h)
    take(0, h)
    rsend[0, first] = acc[first].astype(BF16)
    start_half(True).start()
    lsend[0, second] = acc[second].astype(BF16)
    start_half(False).start()

    _, share, low = v_ref.shape
    batch = 4 * low
    count = down_ref.shape[0] // batch

    def down(i, total):
        every = jnp.dot(down_ref[pl.ds(pl.multiple_of(i * batch, batch), batch), :], y_ref[...],
                        preferred_element_type=F32)
        for j in range(4):
            total = total + jnp.where(tenant_ref[...] == 4 * i + j, every[j * low : (j + 1) * low], 0.0)
        return total

    v_mine = lax.fori_loop(0, count, down, jnp.zeros((low, y_ref.shape[1]), F32))
    v_ref[...] = v_mine.T.reshape(n, share, low)
    vrecv[0] = v_ref[me]

    @pl.loop(1, n)
    def _(d):
        t = lax.rem(me + d, n)
        remote(v_ref.at[t], vrecv.at[d], s1.at[d], r1.at[d], t).start()

    give(1, h - 1)
    give(2, 1 - h)
    take(1, h - 1)
    start_half(True).wait_recv()
    rsend[1, first] = (acc[first] + rrecv[0, first].astype(F32)).astype(BF16)
    rsend[1, second] = acc[second].astype(BF16)
    going(1, True).start()
    take(2, 1 - h)
    start_half(False).wait_recv()
    lsend[1, second] = (acc[second] + lrecv[0, second].astype(F32)).astype(BF16)
    lsend[1, first] = acc[first].astype(BF16)
    going(1, False).start()

    @pl.loop(1, n)
    def _(d):
        remote(v_ref.at[0], vrecv.at[d], s1.at[d], r1.at[d], lax.rem(me + d, n)).wait()

    v_out[me] = jnp.sum(vrecv[...], axis=0).astype(BF16)

    @pl.loop(1, n)
    def _(d):
        remote(v_out.at[me], v_out.at[me], s2.at[d], r2.at[d], lax.rem(me + d, n)).start()

    @pl.loop(2, h)
    def _(s):
        give(2 * s - 1, h - s)
        give(2 * s, s - h)
        take(2 * s - 1, h - s)
        going(s - 1, True).wait_recv()
        rsend[s] = (acc[...] + rrecv[s - 1].astype(F32)).astype(BF16)
        going(s, True).start()
        take(2 * s, s - h)
        going(s - 1, False).wait_recv()
        lsend[s] = (acc[...] + lrecv[s - 1].astype(F32)).astype(BF16)
        going(s, False).start()

    give(m - 1, 0)

    @pl.loop(1, n)
    def _(d):
        t = lax.rem(me + n - d, n)
        remote(v_out.at[t], v_out.at[t], s2.at[d], r2.at[d], t).wait()

    v_all = v_out[...].astype(F32).reshape(n * share, low).T
    more[...] = jnp.zeros_like(more)

    @pl.loop(0, count)
    def _(i):
        wide = jnp.concatenate(
            [jnp.where(tenant_ref[...] == 4 * i + j, v_all, 0.0) for j in range(4)], axis=0)
        more[...] += dot0(up_ref[pl.ds(pl.multiple_of(i * batch, batch), batch), :], wide.astype(BF16))

    take(m - 1, 0)
    more[...] += acc[...]
    going(h - 1, True).wait_recv()
    going(h - 1, False).wait_recv()
    out_ref[...] = (more[...] + rrecv[h - 1].astype(F32) + lrecv[h - 1].astype(F32)).astype(BF16)

    start_half(True).wait_send()
    start_half(False).wait_send()

    @pl.loop(1, h)
    def _(s):
        going(s, True).wait_send()
        going(s, False).wait_send()

    @pl.loop(0, m)
    def _(k):
        sib(k).wait_send()


def conv_kernel(x_ref, cache_ref, land_ref, pick_ref, hit_ref, chan_ref, next_ref, u_ref):
    hit = hit_ref[...] > 0
    count = cache_ref.shape[0]
    chan = chan_ref[...].T
    total = chan[:, count + 1 : count + 2]
    for k in range(count):
        placed = dot0(land_ref[k], pick_ref[...])
        old = jnp.where(hit, placed, cache_ref[k].astype(F32))
        total = total + old * chan[:, k : k + 1]
        if k > 0:
            next_ref[k - 1] = old.astype(BF16)
    low = x_ref[...].astype(BF16)
    next_ref[count - 1] = low
    total = total + low.astype(F32) * chan[:, count : count + 1]
    u_ref[...] = (total / (1.0 + jnp.exp(-total))).astype(BF16)


def state_kernel(dt_ref, proj_ref, chan_ref, u_ref, gate_ref,
                 cache_ref, land_ref, pick_ref, hit_ref, next_ref, y_ref):
    rank, states = proj_ref.shape[0], cache_ref.shape[0]
    chan = chan_ref[...].T
    pre = dot0(proj_ref[...], dt_ref[pl.ds(0, rank), :]) + chan[:, states : states + 1]
    b_in = dt_ref[pl.ds(rank, states), :].astype(F32)
    c_out = dt_ref[pl.ds(rank + states, states), :].astype(F32)
    delta = jnp.maximum(pre, 0.0) + jnp.log1p(jnp.exp(-jnp.abs(pre)))
    u = u_ref[...].astype(F32)
    du = delta * u
    hit = hit_ref[...] > 0
    total = chan[:, states + 1 : states + 2] * u
    for k in range(cache_ref.shape[0]):
        placed = dot0(land_ref[k], pick_ref[...])
        old = jnp.where(hit, placed, cache_ref[k].astype(F32))
        state = jnp.exp(-delta * chan[:, k : k + 1]) * old + du * b_in[k : k + 1, :]
        next_ref[k] = state.astype(BF16)
        total = total + state * c_out[k : k + 1, :]
    gate = gate_ref[...]
    y_ref[...] = (total * (gate / (1.0 + jnp.exp(-gate)))).astype(BF16)


def local(n, snake, hidden, input_conv_weight, input_gate_weight, convolution_taps, convolution_bias,
          step_input_projection, step_norm_gain, step_size_projection, step_size_bias, decay_rates,
          skip, output_weight, adapter_down_maps, adapter_up_maps, tenant, convolution_cache,
          recurrent_cache, incoming_recurrent_states, incoming_conv_states, incoming_buffer_row,
          incoming_slot_index):
    rows, reqs = hidden.shape
    width, chans = input_conv_weight.shape
    rank = step_size_projection.shape[0]
    states = decay_rates.shape[0]
    taps = convolution_cache.shape[0]
    tenants, _, low_rank = adapter_down_maps.shape
    held = incoming_recurrent_states.shape[0]
    m, h = n // 2, n // 4
    share = reqs // n
    sds = jax.ShapeDtypeStruct

    def params(cid):
        return pltpu.CompilerParams(
            collective_id=cid, has_side_effects=True, vmem_limit_bytes=LIMIT)

    conv_rows = -(-held * taps // 16) * 16
    conv_in = incoming_conv_states.reshape(held * taps, n, chans).transpose(1, 0, 2)
    conv_in = jnp.pad(conv_in, ((0, 0), (0, conv_rows - held * taps), (0, 0)))

    x_in, gate_in, land_ssm, land_conv = pl.pallas_call(
        functools.partial(gather_kernel, n, snake),
        name="gather_project",
        out_shape=(sds((chans, reqs), F32), sds((chans, reqs), F32),
                   sds((n, held, states, chans), BF16), sds((n, conv_rows, chans), BF16)),
        in_specs=[VM, ANY, ANY, ANY, ANY],
        out_specs=(VM, VM, ANY, ANY),
        scratch_shapes=[
            pltpu.VMEM((n, rows, reqs), BF16), pltpu.VMEM((width, chans), BF16),
            pltpu.VMEM((width, chans), BF16), DMA((2,)), DMA((3,)),
            DMA((h,)), DMA((h,)), DMA((h,)), DMA((h,)), DMA((m,)), DMA((m,)),
            DMA((n,)), DMA((n,)), DMA((n,)), DMA((n,))],
        compiler_params=params(0),
    )(hidden, input_conv_weight, input_gate_weight, incoming_recurrent_states, conv_in)

    buffers = n * held
    land_ssm = land_ssm.reshape(buffers, states, chans).transpose(1, 0, 2)
    land_conv = land_conv[:, : held * taps].reshape(buffers, taps, chans).transpose(1, 0, 2)
    pick = ((incoming_buffer_row[:, None] == jnp.arange(buffers)[None, :]).astype(F32)).T @ (
        incoming_slot_index[:, None] == jnp.arange(reqs)[None, :]).astype(F32)
    hit = jnp.sum(pick, axis=0, keepdims=True)
    pick = pick.astype(BF16)

    eb = 128
    grid = (chans // eb,)
    whole = lambda *shape: pl.BlockSpec(shape, lambda i: (0,) * len(shape))
    rowb = lambda cols: pl.BlockSpec((eb, cols), lambda i: (i, 0))
    mid = lambda lead, cols: pl.BlockSpec((lead, eb, cols), lambda i: (0, i, 0))
    lastb = lambda lead, m_: pl.BlockSpec((lead, m_, eb), lambda i: (0, 0, i))

    def per_channel(*parts):
        joined = jnp.concatenate([p.astype(F32) for p in parts], axis=0)
        return jnp.pad(joined, ((0, -joined.shape[0] % 8), (0, 0)))

    conv_chan = per_channel(convolution_taps, convolution_bias[None])
    state_chan = per_channel(decay_rates, step_size_bias[None], skip[None])

    conv_next, u = pl.pallas_call(
        conv_kernel,
        name="conv_step",
        grid=grid,
        out_shape=(sds((taps, chans, reqs), BF16), sds((chans, reqs), BF16)),
        in_specs=[rowb(reqs), mid(taps, reqs), lastb(taps, buffers), whole(buffers, reqs),
                  whole(1, reqs), pl.BlockSpec((conv_chan.shape[0], eb), lambda i: (0, i))],
        out_specs=(mid(taps, reqs), rowb(reqs)),
        compiler_params=pltpu.CompilerParams(vmem_limit_bytes=LIMIT),
    )(x_in, convolution_cache, land_conv, pick, hit, conv_chan)

    outs = rank + 2 * states
    mix_part = dot0(u, step_input_projection).astype(BF16).reshape(m, 2, share, outs)
    mixed_in = pl.pallas_call(
        functools.partial(mix_kernel, n, rank),
        name="mix_sum",
        out_shape=sds((n, share, outs), BF16),
        in_specs=[VM, VM],
        out_specs=VM,
        scratch_shapes=[pltpu.VMEM((m, share, outs), BF16), pltpu.VMEM((n, share, outs), BF16),
                        DMA((1,)), DMA((1,))] + [DMA((m,))] * 6,
        compiler_params=params(1),
    )(mix_part, step_norm_gain[None, :])
    mixed_in = mixed_in.reshape(reqs, outs).T

    ssm_next, y = pl.pallas_call(
        state_kernel,
        name="state_step",
        grid=grid,
        out_shape=(sds((states, chans, reqs), BF16), sds((chans, reqs), BF16)),
        in_specs=[whole(outs, reqs), pl.BlockSpec((rank, eb), lambda i: (0, i)),
                  pl.BlockSpec((state_chan.shape[0], eb), lambda i: (0, i)), rowb(reqs), rowb(reqs), mid(states, reqs), lastb(states, buffers),
                  whole(buffers, reqs), whole(1, reqs)],
        out_specs=(mid(states, reqs), rowb(reqs)),
        compiler_params=pltpu.CompilerParams(vmem_limit_bytes=LIMIT),
    )(mixed_in, step_size_projection, state_chan, u,
      gate_in, recurrent_cache, land_ssm, pick, hit)

    down = adapter_down_maps.transpose(0, 2, 1).reshape(tenants * low_rank, chans)
    up = adapter_up_maps.reshape(tenants * low_rank, rows)
    block = pltpu.VMEM((h, rows, reqs), BF16)
    pairs = pltpu.VMEM((m, rows, reqs), BF16)
    mixed = pl.pallas_call(
        functools.partial(scatter_kernel, n, snake),
        name="project_scatter",
        out_shape=sds((rows, reqs), BF16),
        in_specs=[VM, ANY, VM, VM, VM],
        out_specs=VM,
        scratch_shapes=[
            pltpu.VMEM((chans, width), BF16), pltpu.VMEM((rows, reqs), F32),
            pltpu.VMEM((rows, reqs), F32), pltpu.VMEM((n, share, low_rank), F32),
            pltpu.VMEM((n, share, low_rank), BF16), pairs, pairs,
            block, block, block, block, pltpu.VMEM((n, share, low_rank), F32), DMA((1,)),
            DMA((h,)), DMA((h,)), DMA((h,)), DMA((h,)), DMA((m,)), DMA((m,)),
            DMA((n,)), DMA((n,)), DMA((n,)), DMA((n,))],
        compiler_params=params(2),
    )(y, output_weight, down, up, tenant.reshape(1, reqs))
    return mixed, ssm_next, conv_next


def solution(mesh):
    placed = (
        P("tensor", "group"),
        P(None, "tensor"),
        P(None, "tensor"),
        P(None, "tensor"),
        P("tensor"),
        P("tensor", None),
        P(),
        P(None, "tensor"),
        P("tensor"),
        P(None, "tensor"),
        P("tensor"),
        P("tensor", None),
        P(None, "tensor", None),
        P(None, None, "tensor"),
        P("group", None),
        P(None, "tensor", "group"),
        P(None, "tensor", "group"),
        P(("group", "tensor"), None, None),
        P(("group", "tensor"), None, None),
        P("group"),
        P("group"),
    )
    n = mesh.shape["tensor"]
    snake = mesh.shape["group"] == 2
    return jax.shard_map(
        functools.partial(local, n, snake),
        mesh=mesh,
        in_specs=placed,
        out_specs=(P("tensor", "group"), P(None, "tensor", "group"), P(None, "tensor", "group")),
        check_vma=False,
    )
```
